256 devices in a mesh: ctx: 32 (over z, x_hi, core), dp: 8 (over y, x_lo).
Axes of the slice: x: 4 (x_hi: 2, x_lo: 2; x = x_hi * 2 + x_lo), y: 4, z: 8, core: 2. Of those that a mesh axis runs over, the one named last changes fastest.
Arguments:
- query_act: bfloat16 [8, 16384, 512], P('dp', 'ctx'), may hold values from -6 to 6
- key_act: bfloat16 [8, 16384, 512], P('dp', 'ctx'), may hold values from -6 to 6
- value_act: bfloat16 [8, 16384, 512], P('dp', 'ctx'), may hold values from -6 to 6
- filter_taps: bfloat16 [128, 512], replicated, may hold values from -0.5 to 0.5
- grad_out: bfloat16 [8, 16384, 512], P('dp', 'ctx'), may hold values from -6 to 6
Outputs:
- grad_query: bfloat16 [8, 16384, 512], P('dp', 'ctx')
- grad_key: bfloat16 [8, 16384, 512], P('dp', 'ctx')
- grad_value: bfloat16 [8, 16384, 512], P('dp', 'ctx')
- grad_filter: float32 [128, 512], replicated
The draws below stay inside these ranges and needn't reach their ends.
All inputs are finite; a program needn't handle non-finite values.
Results may differ from the reference program's by a relative error of at most 0.0052.
Values may be sent and summed in bfloat16 or wider, within the bound.
No kernel may reach another device: no remote copies, remote signals or barrier semaphores. Data moves between devices by JAX's collectives and lax.ppermute only.
A program may use at most 128 MiB of HBM per device.

```python
import math
import jax
import jax.numpy as jnp
from jax import lax

CH = 512
TAPS = 128
SEQS = 8
LEN = 16384


def block_levels(stream_key, extent, split, low, high):
    loudness, own = 1.0, jax.random.fold_in(stream_key, 6)
    for dim, parts in split:
        heights = jnp.exp(jax.random.uniform(jax.random.fold_in(own, dim), (parts,), jnp.float32, low / len(split), high / len(split)))
        loudness = loudness * jnp.repeat(heights, extent[dim] // parts).reshape([-1 if axis == dim else 1 for axis in range(len(extent))])
    return loudness


def gaussian(key, dims, spread, most, pieces=(), kind=jnp.bfloat16):
    factor_of = block_levels(key, dims, pieces, -0.22, 0.18) if pieces else 1.0
    drawn = jax.random.normal(key, dims, jnp.float32) * spread * factor_of
    return jnp.minimum(jnp.maximum(drawn, -most), most).astype(kind)


def setup_inputs(seed: int = 0) -> dict:
    key_of = jax.random.split(jax.random.key(seed), 6)
    query_act = gaussian(key_of[0], (SEQS, LEN, CH), 1.0, 6.0, ((0, 8), (1, 32)))
    key_act = gaussian(key_of[1], (SEQS, LEN, CH), 1.0, 6.0, ((0, 8), (1, 32)))
    value_act = gaussian(key_of[2], (SEQS, LEN, CH), 1.0, 6.0, ((0, 8), (1, 32)))
    filter_taps = gaussian(key_of[3], (TAPS, CH), TAPS ** -0.5, 0.5)
    grad_out = gaussian(key_of[4], (SEQS, LEN, CH), 1.0, 6.0, ((0, 8), (1, 32)))
    return dict(query_act=query_act, key_act=key_act, value_act=value_act, filter_taps=filter_taps, grad_out=grad_out)


def toeplitz_pair(filter_taps):
    offsets = jnp.arange(TAPS)[:, None] - jnp.arange(TAPS)[None, :]
    picked = filter_taps.astype(jnp.float32)[jnp.mod(offsets, TAPS)]
    zeroed = jnp.zeros_like(picked)
    lower = jnp.where((offsets >= 0)[:, :, None], picked, zeroed).transpose(2, 0, 1)
    upper = jnp.where((offsets < 0)[:, :, None], picked, zeroed).transpose(2, 0, 1)
    return (lower, upper)

def reference(query_act, key_act, value_act, filter_taps, grad_out):
    lower, upper = toeplitz_pair(filter_taps)
    block_count = LEN // TAPS
    highest = lax.Precision.HIGHEST

    def one_sequence(accum, inputs):
        query_seq, key_seq, value_seq, grad_seq = inputs
        gated_low = lax.optimization_barrier((key_seq.astype(jnp.float32) * value_seq.astype(jnp.float32)).astype(jnp.bfloat16))
        mix_low = lax.optimization_barrier((grad_seq.astype(jnp.float32) * query_seq.astype(jnp.float32)).astype(jnp.bfloat16))
        gated = gated_low.astype(jnp.float32).reshape(block_count, TAPS, CH)
        mix_grad = mix_low.astype(jnp.float32).reshape(block_count, TAPS, CH)
        zero_block = jnp.zeros((1, TAPS, CH), jnp.float32)
        prior = jnp.concatenate([zero_block, gated[:-1]], axis=0)
        later = jnp.concatenate([mix_grad[1:], zero_block], axis=0)
        mixed = jnp.einsum('nbc,cab->nac', gated, lower, precision=highest) + jnp.einsum('nbc,cab->nac', prior, upper, precision=highest)
        carried = jnp.einsum('nbc,cba->nac', mix_grad, lower, precision=highest) + jnp.einsum('nbc,cba->nac', later, upper, precision=highest)
        windows = jnp.concatenate([prior, gated], axis=1)
        accum = accum + jnp.einsum('nac,nbc->cab', mix_grad, windows, precision=highest)
        mixed = mixed.reshape(LEN, CH)
        carried = carried.reshape(LEN, CH)
        grad_q = (grad_seq.astype(jnp.float32) * mixed).astype(jnp.bfloat16)
        grad_k = (carried * value_seq.astype(jnp.float32)).astype(jnp.bfloat16)
        grad_v = (carried * key_seq.astype(jnp.float32)).astype(jnp.bfloat16)
        return (accum, (grad_q, grad_k, grad_v))
    start_acc = jnp.zeros((CH, TAPS, 2 * TAPS), jnp.float32)
    accum, (grad_query, grad_key, grad_value) = lax.scan(one_sequence, start_acc, (query_act, key_act, value_act, grad_out))
    row_ids = jnp.arange(TAPS)[:, None, None]
    col_ids = jnp.arange(2 * TAPS)[None, :, None]
    tap_ids = jnp.arange(TAPS)[None, None, :]
    selector = (col_ids == row_ids + TAPS - tap_ids).astype(jnp.float32)
    summed = jnp.einsum('cab,abj->jc', accum, selector, precision=highest)
    grad_filter = summed / math.sqrt(SEQS * LEN)
    return (grad_query, grad_key, grad_value, grad_filter)
```

```python
import functools
import math

import jax
import jax.numpy as jnp
import ml_dtypes
import numpy as np
from jax import lax
from jax.experimental import pallas as pl
from jax.experimental.pallas import tpu as pltpu
from jax.sharding import Mesh, PartitionSpec as P

F32 = jnp.float32
BF16 = jnp.bfloat16
BLOCK = 128
SPEC = 256
HALF = BLOCK // 2
WIDTH = 256
VMEM_LIMIT = 40 * 1024 * 1024


def split_in_two(matrix):
    high = matrix.astype(ml_dtypes.bfloat16)
    low = (matrix - high.astype(np.float64)).astype(ml_dtypes.bfloat16)
    return high, low


def transform_matrices():
    freqs = np.concatenate([np.arange(0, BLOCK, 2), np.arange(1, BLOCK, 2)])
    angles = 2 * np.pi * freqs[:, None] * np.arange(BLOCK)[None, :] / SPEC
    real, imag = np.cos(angles), -np.sin(angles)
    imag[0] = np.cos(np.pi * np.arange(BLOCK))
    forward = np.concatenate([real, imag], axis=0)
    weight = np.full((SPEC,), 2.0 / SPEC)
    weight[0] = weight[BLOCK] = 1.0 / SPEC
    inverse = (forward * weight[:, None]).T
    return (
        np.concatenate(split_in_two(forward), axis=1),
        np.concatenate(split_in_two(inverse), axis=1),
    )


def dot(left, right):
    return jnp.dot(left, right, preferred_element_type=F32)


def spectrum(forward, block):
    both = dot(forward, jnp.concatenate([block, block], axis=0))
    return both[:BLOCK], both[BLOCK:]


def inverse_of(inverse, real, imag):
    both = jnp.concatenate([real, imag], axis=0)
    high = both.astype(BF16)
    low = (both - high.astype(F32)).astype(BF16)
    return dot(inverse, jnp.concatenate([high, high], axis=0)) + dot(inverse[:, :SPEC], low)


def beside(first, second):
    def joined(a, b):
        return jnp.concatenate([a[:HALF] + b[:HALF], a[HALF:] - b[HALF:]], axis=0)

    return joined(first[0], second[0]), joined(first[1], second[1])


def first_row(shape):
    return lax.broadcasted_iota(jnp.int32, shape, 0) == 0


def product(left, right):
    return (left.astype(F32) * right.astype(F32)).astype(BF16)


def rows(ref, block):
    return ref[0, pl.ds(block * BLOCK, BLOCK), :]


def correlation_terms(grad, gated):
    real = grad[0] * gated[0]
    imag = grad[1] * gated[1]
    cross = grad[1] * gated[0] - grad[0] * gated[1]
    return real, imag, cross


def correlation(inverse, terms):
    real, imag, cross = terms
    top = first_row(real.shape)
    return inverse_of(
        inverse, real + jnp.where(top, 0.0, imag), jnp.where(top, imag, cross)
    )


def edge_kernel(key_ref, value_ref, query_ref, grad_ref, gated_ref, mix_ref):
    gated_ref[...] = product(key_ref[0], value_ref[0])
    mix_ref[...] = product(query_ref[0], grad_ref[0])


def inner_kernel(query_ref, key_ref, value_ref, grad_ref, fwd_ref, inv_ref, out_ref):
    fwd = fwd_ref[...]
    blocks = query_ref.shape[1] // BLOCK
    terms = None
    before = None
    for n in range(blocks):
        gated = spectrum(fwd, product(rows(key_ref, n), rows(value_ref, n)))
        grad = spectrum(fwd, product(rows(query_ref, n), rows(grad_ref, n)))
        window = gated if before is None else beside(gated, before)
        more = correlation_terms(grad, window)
        terms = more if terms is None else tuple(a + b for a, b in zip(terms, more))
        before = gated
    out_ref[...] = correlation(inv_ref[...], terms)


def outer_kernel(halo_ref, mix_ref, inner_ref, fwd_ref, inv_ref, out_ref):
    fwd = fwd_ref[...]
    halo = spectrum(fwd, halo_ref[...])
    zero = jnp.zeros_like(halo[0])
    window = beside((zero, zero), halo)
    grad = spectrum(fwd, mix_ref[...])
    total = inner_ref[...] + correlation(inv_ref[...], correlation_terms(grad, window))
    for part in range(total.shape[1] // 128):
        out_ref[pl.ds(part * BLOCK, BLOCK), :] = total[:, part * 128 : (part + 1) * 128].astype(BF16)


def conv_kernel(
    query_ref, key_ref, value_ref, grad_ref, before_ref, after_ref, taps_ref, fwd_ref, inv_ref,
    out_query_ref, out_key_ref, out_value_ref,
):
    fwd, inv = fwd_ref[...], inv_ref[...]
    blocks = query_ref.shape[1] // BLOCK
    real, imag = spectrum(fwd, taps_ref[...])
    top = first_row(real.shape)
    cross = jnp.where(top, 0.0, imag)
    last = jnp.where(top, imag, real)
    before = spectrum(fwd, before_ref[...])
    for n in range(blocks):
        gated = spectrum(fwd, product(rows(key_ref, n), rows(value_ref, n)))
        wr, wi = beside(gated, before)
        mixed = inverse_of(inv, wr * real - wi * cross, wr * cross + wi * last)
        out_query_ref[0, pl.ds(n * BLOCK, BLOCK), :] = (
            rows(grad_ref, n).astype(F32) * mixed
        ).astype(BF16)
        before = gated
    after = spectrum(fwd, after_ref[...])
    for n in reversed(range(blocks)):
        grad = spectrum(fwd, product(rows(query_ref, n), rows(grad_ref, n)))
        wr, wi = beside(grad, after)
        carried = inverse_of(inv, wr * real + wi * cross, wi * last - wr * cross)
        out_key_ref[0, pl.ds(n * BLOCK, BLOCK), :] = (
            carried * rows(value_ref, n).astype(F32)
        ).astype(BF16)
        out_value_ref[0, pl.ds(n * BLOCK, BLOCK), :] = (
            carried * rows(key_ref, n).astype(F32)
        ).astype(BF16)
        after = grad


def params():
    return pltpu.CompilerParams(vmem_limit_bytes=VMEM_LIMIT)


def cost(flops, moved):
    return pl.CostEstimate(flops=flops, bytes_accessed=moved, transcendentals=0)


def shards(query_act, key_act, value_act, filter_taps, grad_out, count_all=1):
    _, row_count, chan_count = query_act.shape
    blocks = row_count // BLOCK
    steps = chan_count // WIDTH
    fwd_np, inv_np = transform_matrices()
    fwd, inv = jnp.asarray(fwd_np), jnp.asarray(inv_np)

    whole = pl.BlockSpec((1, row_count, WIDTH), lambda i: (0, 0, i))
    slab = pl.BlockSpec((BLOCK, WIDTH), lambda i: (0, i))
    fwd_spec = pl.BlockSpec(fwd.shape, lambda i: (0, 0))
    inv_spec = pl.BlockSpec(inv.shape, lambda i: (0, 0))

    last_rows = pl.BlockSpec((1, BLOCK, chan_count), lambda i: (0, blocks - 1, 0))
    first_rows = pl.BlockSpec((1, BLOCK, chan_count), lambda i: (0, 0, 0))
    edge = pl.BlockSpec((BLOCK, chan_count), lambda i: (0, 0))
    edge_shape = jax.ShapeDtypeStruct((BLOCK, chan_count), BF16)
    gated_edge, mix_edge = pl.pallas_call(
        edge_kernel,
        grid=(1,),
        in_specs=[last_rows, last_rows, first_rows, first_rows],
        out_specs=[edge, edge],
        out_shape=[edge_shape, edge_shape],
        compiler_params=params(),
        cost_estimate=cost(200_000, 800_000),
        name="edges",
    )(key_act, value_act, query_act, grad_out)

    ctx = ("z", "xh", "c")
    ring = 1
    for name in ctx:
        ring *= lax.axis_size(name)
    before = lax.ppermute(gated_edge, ctx, [(i, i + 1) for i in range(ring - 1)])
    after = lax.ppermute(mix_edge, ctx, [(i + 1, i) for i in range(ring - 1)])

    inner = pl.pallas_call(
        inner_kernel,
        grid=(steps,),
        in_specs=[whole, whole, whole, whole, fwd_spec, inv_spec],
        out_specs=slab,
        out_shape=jax.ShapeDtypeStruct((BLOCK, chan_count), F32),
        compiler_params=params(),
        cost_estimate=cost(800_000_000, 2_500_000),
        name="inner_pairs",
    )(query_act, key_act, value_act, grad_out, fwd, inv)

    partial = pl.pallas_call(
        outer_kernel,
        grid=(steps,),
        in_specs=[slab, slab, slab, fwd_spec, inv_spec],
        out_specs=pl.BlockSpec((BLOCK * WIDTH // 128, 128), lambda i: (i, 0)),
        out_shape=jax.ShapeDtypeStruct((BLOCK * chan_count // 128, 128), BF16),
        compiler_params=params(),
        cost_estimate=cost(200_000_000, 800_000),
        name="outer_pairs",
    )(before, mix_edge, inner, fwd, inv)

    near = ("xh", "c", "y", "xl")
    near_count = 1
    for name in near:
        near_count *= lax.axis_size(name)
    far = "z"
    far_count = lax.axis_size(far)
    chunks = partial.reshape(near_count, -1, 128)
    mine = lax.all_to_all(chunks, near, 0, 0, tiled=True).astype(F32).sum(axis=0)
    planes = jnp.broadcast_to(mine[None], (far_count,) + mine.shape)
    mine = lax.all_to_all(planes, far, 0, 0, tiled=True).sum(axis=0) / math.sqrt(count_all)
    copies = jnp.broadcast_to(mine.astype(BF16)[None], (near_count,) + mine.shape)
    total = lax.all_to_all(copies, near, 0, 0, tiled=True)
    total = total.reshape(chan_count // 128, BLOCK, 128).astype(F32)
    grad_filter = jnp.concatenate([total[i] for i in range(chan_count // 128)], axis=1)

    out_shape = jax.ShapeDtypeStruct(query_act.shape, BF16)
    grad_query, grad_key, grad_value = pl.pallas_call(
        conv_kernel,
        grid=(steps,),
        in_specs=[whole, whole, whole, whole, slab, slab, slab, fwd_spec, inv_spec],
        out_specs=[whole, whole, whole],
        out_shape=[out_shape, out_shape, out_shape],
        compiler_params=params(),
        cost_estimate=cost(2_000_000_000, 4_000_000),
        name="convolutions",
    )(query_act, key_act, value_act, grad_out, before, after, filter_taps, fwd, inv)
    return grad_query, grad_key, grad_value, grad_filter


def solution(mesh):
    fine = Mesh(mesh.devices.reshape(8, 2, 2, 4, 2), ("z", "xh", "c", "y", "xl"))
    spec = P(("y", "xl"), ("z", "xh", "c"), None)

    def whole(query_act, key_act, value_act, filter_taps, grad_out):
        count_all = query_act.shape[0] * query_act.shape[1]
        return jax.shard_map(
            functools.partial(shards, count_all=count_all),
            mesh=fine,
            in_specs=(spec, spec, spec, P(), spec),
            out_specs=(spec, spec, spec, P()),
            check_vma=False,
        )(query_act, key_act, value_act, filter_taps, grad_out)

    return whole
```

```python
import functools
import math

import jax
import jax.numpy as jnp
import ml_dtypes
import numpy as np
from jax import lax
from jax.experimental import pallas as pl
from jax.experimental.pallas import tpu as pltpu
from jax.sharding import Mesh, PartitionSpec as P

F32 = jnp.float32
BF16 = jnp.bfloat16
BLOCK = 128
SPEC = 256
HALF = BLOCK // 2
WIDTH = 256
VMEM_LIMIT = 40 * 1024 * 1024


def split_in_two(matrix):
    high = matrix.astype(ml_dtypes.bfloat16)
    low = (matrix - high.astype(np.float64)).astype(ml_dtypes.bfloat16)
    return high, low


def transform_matrices():
    freqs = np.concatenate([np.arange(0, BLOCK, 2), np.arange(1, BLOCK, 2)])
    angles = 2 * np.pi * freqs[:, None] * np.arange(BLOCK)[None, :] / SPEC
    real, imag = np.cos(angles), -np.sin(angles)
    imag[0] = np.cos(np.pi * np.arange(BLOCK))
    forward = np.concatenate([real, imag], axis=0)
    weight = np.full((SPEC,), 2.0 / SPEC)
    weight[0] = weight[BLOCK] = 1.0 / SPEC
    inverse = (forward * weight[:, None]).T
    return (
        np.concatenate(split_in_two(forward), axis=1),
        np.concatenate(split_in_two(inverse), axis=1),
    )


def dot(left, right):
    return jnp.dot(left, right, preferred_element_type=F32)


def spectrum(forward, block):
    both = dot(forward, jnp.concatenate([block, block], axis=0))
    return both[:BLOCK], both[BLOCK:]


def inverse_of(inverse, real, imag):
    both = jnp.concatenate([real, imag], axis=0)
    high = both.astype(BF16)
    low = (both - high.astype(F32)).astype(BF16)
    return dot(inverse, jnp.concatenate([high, high], axis=0)) + dot(inverse[:, :SPEC], low)


def beside(first, second):
    def joined(a, b):
        return jnp.concatenate([a[:HALF] + b[:HALF], a[HALF:] - b[HALF:]], axis=0)

    return joined(first[0], second[0]), joined(first[1], second[1])


def first_row(shape):
    return lax.broadcasted_iota(jnp.int32, shape, 0) == 0


def product(left, right):
    return (left.astype(F32) * right.astype(F32)).astype(BF16)


def rows(block):
    return pl.ds(block * BLOCK, BLOCK)


def correlation_terms(grad, gated):
    real = grad[0] * gated[0]
    imag = grad[1] * gated[1]
    cross = grad[1] * gated[0] - grad[0] * gated[1]
    return real, imag, cross


def correlation(inverse, terms):
    real, imag, cross = terms
    top = first_row(real.shape)
    return inverse_of(
        inverse, real + jnp.where(top, 0.0, imag), jnp.where(top, imag, cross)
    )


def inner_kernel(gated_ref, mix_ref, fwd_ref, inv_ref, out_ref):
    fwd = fwd_ref[...]
    blocks = gated_ref.shape[0] // BLOCK
    terms = None
    before = None
    for n in range(blocks):
        gated = spectrum(fwd, gated_ref[rows(n), :])
        grad = spectrum(fwd, mix_ref[rows(n), :])
        window = gated if before is None else beside(gated, before)
        more = correlation_terms(grad, window)
        terms = more if terms is None else tuple(a + b for a, b in zip(terms, more))
        before = gated
    out_ref[...] = correlation(inv_ref[...], terms)


def outer_kernel(halo_ref, mix_ref, inner_ref, fwd_ref, inv_ref, out_ref):
    fwd = fwd_ref[...]
    halo = spectrum(fwd, halo_ref[...])
    zero = jnp.zeros_like(halo[0])
    window = beside((zero, zero), halo)
    grad = spectrum(fwd, mix_ref[...])
    total = inner_ref[...] + correlation(inv_ref[...], correlation_terms(grad, window))
    for part in range(total.shape[1] // 128):
        out_ref[pl.ds(part * BLOCK, BLOCK), :] = total[:, part * 128 : (part + 1) * 128].astype(BF16)


def conv_kernel(
    gated_ref, mix_ref, key_ref, value_ref, grad_ref, before_ref, after_ref, taps_ref, fwd_ref, inv_ref,
    out_query_ref, out_key_ref, out_value_ref,
):
    fwd, inv = fwd_ref[...], inv_ref[...]
    blocks = gated_ref.shape[0] // BLOCK
    real, imag = spectrum(fwd, taps_ref[...])
    top = first_row(real.shape)
    cross = jnp.where(top, 0.0, imag)
    last = jnp.where(top, imag, real)
    before = spectrum(fwd, before_ref[...])
    for n in range(blocks):
        gated = spectrum(fwd, gated_ref[rows(n), :])
        wr, wi = beside(gated, before)
        mixed = inverse_of(inv, wr * real - wi * cross, wr * cross + wi * last)
        out_query_ref[0, rows(n), :] = (grad_ref[0, rows(n), :].astype(F32) * mixed).astype(BF16)
        before = gated
    after = spectrum(fwd, after_ref[...])
    for n in reversed(range(blocks)):
        grad = spectrum(fwd, mix_ref[rows(n), :])
        wr, wi = beside(grad, after)
        carried = inverse_of(inv, wr * real + wi * cross, wi * last - wr * cross)
        out_key_ref[0, rows(n), :] = (carried * value_ref[0, rows(n), :].astype(F32)).astype(BF16)
        out_value_ref[0, rows(n), :] = (carried * key_ref[0, rows(n), :].astype(F32)).astype(BF16)
        after = grad


def params():
    return pltpu.CompilerParams(vmem_limit_bytes=VMEM_LIMIT)


def cost(flops, moved):
    return pl.CostEstimate(flops=flops, bytes_accessed=moved, transcendentals=0)


def shards(query_act, key_act, value_act, filter_taps, grad_out, count_all=1):
    _, row_count, chan_count = query_act.shape
    blocks = row_count // BLOCK
    steps = chan_count // WIDTH
    fwd_np, inv_np = transform_matrices()
    fwd, inv = jnp.asarray(fwd_np), jnp.asarray(inv_np)

    whole = pl.BlockSpec((1, row_count, WIDTH), lambda i: (0, 0, i))
    stack = pl.BlockSpec((row_count, WIDTH), lambda i: (0, i))
    slab = pl.BlockSpec((BLOCK, WIDTH), lambda i: (0, i))
    fwd_spec = pl.BlockSpec(fwd.shape, lambda i: (0, 0))
    inv_spec = pl.BlockSpec(inv.shape, lambda i: (0, 0))

    gated = product(key_act[0], value_act[0])
    mix = product(query_act[0], grad_out[0])

    ctx = ("z", "xh", "c")
    ring = 1
    for name in ctx:
        ring *= lax.axis_size(name)
    before = lax.ppermute(gated[row_count - BLOCK :], ctx, [(i, i + 1) for i in range(ring - 1)])
    after = lax.ppermute(mix[:BLOCK], ctx, [(i + 1, i) for i in range(ring - 1)])

    inner = pl.pallas_call(
        inner_kernel,
        grid=(steps,),
        in_specs=[stack, stack, fwd_spec, inv_spec],
        out_specs=slab,
        out_shape=jax.ShapeDtypeStruct((BLOCK, chan_count), F32),
        compiler_params=params(),
        cost_estimate=cost(800_000_000, 2_500_000),
        name="inner_pairs",
    )(gated, mix, fwd, inv)

    partial = pl.pallas_call(
        outer_kernel,
        grid=(steps,),
        in_specs=[slab, slab, slab, fwd_spec, inv_spec],
        out_specs=pl.BlockSpec((BLOCK * WIDTH // 128, 128), lambda i: (i, 0)),
        out_shape=jax.ShapeDtypeStruct((BLOCK * chan_count // 128, 128), BF16),
        compiler_params=params(),
        cost_estimate=cost(200_000_000, 800_000),
        name="outer_pairs",
    )(before, mix, inner, fwd, inv)

    near = ("xh", "c", "y", "xl")
    near_count = 1
    for name in near:
        near_count *= lax.axis_size(name)
    far = "z"
    far_count = lax.axis_size(far)
    chunks = partial.reshape(near_count, -1, 128)
    mine = lax.all_to_all(chunks, near, 0, 0, tiled=True).astype(F32).sum(axis=0)
    out_shape = jax.ShapeDtypeStruct(query_act.shape, BF16)
    grad_query, grad_key, grad_value = pl.pallas_call(
        conv_kernel,
        grid=(steps,),
        in_specs=[stack, stack, whole, whole, whole, slab, slab, slab, fwd_spec, inv_spec],
        out_specs=[whole, whole, whole],
        out_shape=[out_shape, out_shape, out_shape],
        compiler_params=params(),
        cost_estimate=cost(2_000_000_000, 4_000_000),
        name="convolutions",
    )(gated, mix, key_act, value_act, grad_out, before, after, filter_taps, fwd, inv)
    mine, grad_query, grad_key, grad_value = lax.optimization_barrier(
        (mine, grad_query, grad_key, grad_value)
    )
    planes = jnp.broadcast_to(mine[None], (far_count,) + mine.shape)
    mine = lax.all_to_all(planes, far, 0, 0, tiled=True).sum(axis=0) / math.sqrt(count_all)
    copies = jnp.broadcast_to(mine.astype(BF16)[None], (near_count,) + mine.shape)
    total = lax.all_to_all(copies, near, 0, 0, tiled=True)
    total = total.reshape(chan_count // 128, BLOCK, 128).astype(F32)
    grad_filter = jnp.concatenate([total[i] for i in range(chan_count // 128)], axis=1)

    return grad_query, grad_key, grad_value, grad_filter


def solution(mesh):
    fine = Mesh(mesh.devices.reshape(8, 2, 2, 4, 2), ("z", "xh", "c", "y", "xl"))
    spec = P(("y", "xl"), ("z", "xh", "c"), None)

    def whole(query_act, key_act, value_act, filter_taps, grad_out):
        count_all = query_act.shape[0] * query_act.shape[1]
        return jax.shard_map(
            functools.partial(shards, count_all=count_all),
            mesh=fine,
            in_specs=(spec, spec, spec, P(), spec),
            out_specs=(spec, spec, spec, P()),
            check_vma=False,
        )(query_act, key_act, value_act, filter_taps, grad_out)

    return whole
```

```python
import functools
import math

import jax
import jax.numpy as jnp
import ml_dtypes
import numpy as np
from jax import lax
from jax.experimental import pallas as pl
from jax.experimental.pallas import tpu as pltpu
from jax.sharding import Mesh, PartitionSpec as P

F32 = jnp.float32
BF16 = jnp.bfloat16
BLOCK = 128
SPEC = 256
HALF = BLOCK // 2
WIDTH = 256
VMEM_LIMIT = 40 * 1024 * 1024


def split_in_two(matrix):
    high = matrix.astype(ml_dtypes.bfloat16)
    low = (matrix - high.astype(np.float64)).astype(ml_dtypes.bfloat16)
    return high, low


def transform_matrices():
    freqs = np.concatenate([np.arange(0, BLOCK, 2), np.arange(1, BLOCK, 2)])
    angles = 2 * np.pi * freqs[:, None] * np.arange(BLOCK)[None, :] / SPEC
    real, imag = np.cos(angles), -np.sin(angles)
    imag[0] = np.cos(np.pi * np.arange(BLOCK))
    forward = np.concatenate([real, imag], axis=0)
    weight = np.full((SPEC,), 2.0 / SPEC)
    weight[0] = weight[BLOCK] = 1.0 / SPEC
    inverse = (forward * weight[:, None]).T
    return (
        np.concatenate(split_in_two(forward), axis=1),
        np.concatenate(split_in_two(inverse), axis=0),
    )


def dot(left, right):
    return jnp.dot(left, right, preferred_element_type=F32)


def spectrum(forward, block):
    both = dot(forward, jnp.concatenate([block, block], axis=0))
    return both[:BLOCK], both[BLOCK:]


def inverse_of(inverse, real, imag):
    both = jnp.concatenate([real, imag], axis=0)
    high = both.astype(BF16)
    low = (both - high.astype(F32)).astype(BF16)
    terms = dot(inverse, high)
    return terms[:BLOCK] + terms[BLOCK:] + dot(inverse[:BLOCK], low)


def beside(first, second):
    def joined(a, b):
        return jnp.concatenate([a[:HALF] + b[:HALF], a[HALF:] - b[HALF:]], axis=0)

    return joined(first[0], second[0]), joined(first[1], second[1])


def first_row(shape):
    return lax.broadcasted_iota(jnp.int32, shape, 0) == 0


def product(left, right):
    return (left.astype(F32) * right.astype(F32)).astype(BF16)


def rows(block):
    return pl.ds(block * BLOCK, BLOCK)


def correlation_terms(grad, gated):
    real = grad[0] * gated[0]
    imag = grad[1] * gated[1]
    cross = grad[1] * gated[0] - grad[0] * gated[1]
    return real, imag, cross


def correlation(inverse, terms):
    real, imag, cross = terms
    top = first_row(real.shape)
    return inverse_of(
        inverse, real + jnp.where(top, 0.0, imag), jnp.where(top, imag, cross)
    )


def inner_kernel(gated_ref, mix_ref, fwd_ref, inv_ref, out_ref):
    fwd, inv = fwd_ref[...], inv_ref[...]
    blocks = gated_ref.shape[0] // BLOCK
    for part in range(gated_ref.shape[1] // WIDTH):
        chans = pl.ds(part * WIDTH, WIDTH)
        terms = None
        before = None
        for n in range(blocks):
            gated = spectrum(fwd, gated_ref[rows(n), chans])
            grad = spectrum(fwd, mix_ref[rows(n), chans])
            window = gated if before is None else beside(gated, before)
            more = correlation_terms(grad, window)
            terms = more if terms is None else tuple(a + b for a, b in zip(terms, more))
            before = gated
        out_ref[:, chans] = correlation(inv, terms)


def outer_kernel(halo_ref, mix_ref, inner_ref, fwd_ref, inv_ref, out_ref):
    fwd, inv = fwd_ref[...], inv_ref[...]
    for part in range(halo_ref.shape[1] // WIDTH):
        chans = pl.ds(part * WIDTH, WIDTH)
        halo = spectrum(fwd, halo_ref[:, chans])
        zero = jnp.zeros_like(halo[0])
        window = beside((zero, zero), halo)
        grad = spectrum(fwd, mix_ref[:, chans])
        total = inner_ref[:, chans] + correlation(inv, correlation_terms(grad, window))
        for piece in range(WIDTH // 128):
            out_ref[rows(part * (WIDTH // 128) + piece), :] = total[
                :, piece * 128 : (piece + 1) * 128
            ].astype(BF16)


def conv_kernel(
    gated_ref, mix_ref, key_ref, value_ref, grad_ref, before_ref, after_ref, taps_ref, fwd_ref, inv_ref,
    out_query_ref, out_key_ref, out_value_ref,
):
    fwd, inv = fwd_ref[...], inv_ref[...]
    blocks = gated_ref.shape[0] // BLOCK
    real, imag = spectrum(fwd, taps_ref[...])
    top = first_row(real.shape)
    cross = jnp.where(top, 0.0, imag)
    last = jnp.where(top, imag, real)

    def backward(n, grad, after):
        wr, wi = beside(grad, after)
        carried = inverse_of(inv, wr * real + wi * cross, wi * last - wr * cross)
        out_key_ref[0, rows(n), :] = (carried * value_ref[0, rows(n), :].astype(F32)).astype(BF16)
        out_value_ref[0, rows(n), :] = (carried * key_ref[0, rows(n), :].astype(F32)).astype(BF16)

    before = spectrum(fwd, before_ref[...])
    earlier = None
    for n in range(blocks):
        gated = spectrum(fwd, gated_ref[rows(n), :])
        grad = spectrum(fwd, mix_ref[rows(n), :])
        wr, wi = beside(gated, before)
        mixed = inverse_of(inv, wr * real - wi * cross, wr * cross + wi * last)
        out_query_ref[0, rows(n), :] = (grad_ref[0, rows(n), :].astype(F32) * mixed).astype(BF16)
        if earlier is not None:
            backward(n - 1, earlier, grad)
        before, earlier = gated, grad
    backward(blocks - 1, earlier, spectrum(fwd, after_ref[...]))


def params():
    return pltpu.CompilerParams(vmem_limit_bytes=VMEM_LIMIT)


def cost(flops, moved):
    return pl.CostEstimate(flops=flops, bytes_accessed=moved, transcendentals=0)


def shards(query_act, key_act, value_act, filter_taps, grad_out, count_all=1):
    _, row_count, chan_count = query_act.shape
    blocks = row_count // BLOCK
    fwd_np, inv_np = transform_matrices()
    fwd, inv = jnp.asarray(fwd_np), jnp.asarray(inv_np)

    whole = pl.BlockSpec((1, row_count, chan_count), lambda i: (0, 0, 0))
    stack = pl.BlockSpec((row_count, chan_count), lambda i: (0, 0))
    slab = pl.BlockSpec((BLOCK, chan_count), lambda i: (0, 0))
    fwd_spec = pl.BlockSpec(fwd.shape, lambda i: (0, 0))
    inv_spec = pl.BlockSpec(inv.shape, lambda i: (0, 0))

    gated = product(key_act[0], value_act[0])
    mix = product(query_act[0], grad_out[0])

    ctx = ("z", "xh", "c")
    ring = 1
    for name in ctx:
        ring *= lax.axis_size(name)
    gated_edge, mix_edge = gated[row_count - BLOCK :], mix[:BLOCK]
    first_core = lax.axis_index("c") == 0
    inside = [(i, i + 1) for i in range(0, ring - 1, 2)]
    outside = [(i, i + 1) for i in range(1, ring - 1, 2)]
    both_ways = [pairs + [(j, i) for i, j in pairs] for pairs in (inside, outside)]
    from_inside = lax.ppermute(jnp.where(first_core, gated_edge, mix_edge), ctx, both_ways[0])
    to_outside = jnp.where(
        first_core,
        product(query_act[0, :BLOCK], grad_out[0, :BLOCK]),
        product(key_act[0, row_count - BLOCK :], value_act[0, row_count - BLOCK :]),
    )
    from_outside = lax.ppermute(to_outside, ctx, both_ways[1])
    before = jnp.where(first_core, from_outside, from_inside)
    after = jnp.where(first_core, from_inside, from_outside)

    close = pl.BlockSpec(memory_space=pltpu.VMEM)
    inner = pl.pallas_call(
        inner_kernel,
        in_specs=[close] * 4,
        out_specs=close,
        out_shape=jax.ShapeDtypeStruct((BLOCK, chan_count), F32),
        compiler_params=params(),
        cost_estimate=cost(800_000_000, 2_500_000),
        name="inner_pairs",
    )(gated, mix, fwd, inv)

    partial = pl.pallas_call(
        outer_kernel,
        in_specs=[close] * 5,
        out_specs=close,
        out_shape=jax.ShapeDtypeStruct((BLOCK * chan_count // 128, 128), BF16),
        compiler_params=params(),
        cost_estimate=cost(200_000_000, 800_000),
        name="outer_pairs",
    )(before, mix_edge, inner, fwd, inv)

    near = ("xh", "c", "y", "xl")
    near_count = 1
    for name in near:
        near_count *= lax.axis_size(name)
    far = "z"
    far_count = lax.axis_size(far)
    chunks = partial.reshape(near_count, -1, 128)
    mine = lax.all_to_all(chunks, near, 0, 0, tiled=True).astype(F32).sum(axis=0)
    out_shape = jax.ShapeDtypeStruct(query_act.shape, BF16)
    grad_query, grad_key, grad_value = pl.pallas_call(
        conv_kernel,
        grid=(1,),
        in_specs=[stack, stack, whole, whole, whole, slab, slab, slab, fwd_spec, inv_spec],
        out_specs=[whole, whole, whole],
        out_shape=[out_shape, out_shape, out_shape],
        compiler_params=params(),
        cost_estimate=cost(2_000_000_000, 4_000_000),
        name="convolutions",
    )(gated, mix, key_act, value_act, grad_out, before, after, filter_taps, fwd, inv)
    mine, grad_query, grad_key, grad_value = lax.optimization_barrier(
        (mine, grad_query, grad_key, grad_value)
    )
    planes = jnp.broadcast_to(mine[None], (far_count,) + mine.shape)
    mine = lax.all_to_all(planes, far, 0, 0, tiled=True).sum(axis=0) / math.sqrt(count_all)
    copies = jnp.broadcast_to(mine.astype(BF16)[None], (near_count,) + mine.shape)
    total = lax.all_to_all(copies, near, 0, 0, tiled=True)
    total = total.reshape(chan_count // 128, BLOCK, 128).astype(F32)
    grad_filter = jnp.concatenate([total[i] for i in range(chan_count // 128)], axis=1)

    return grad_query, grad_key, grad_value, grad_filter


def solution(mesh):
    fine = Mesh(mesh.devices.reshape(8, 2, 2, 4, 2), ("z", "xh", "c", "y", "xl"))
    spec = P(("y", "xl"), ("z", "xh", "c"), None)

    def whole(query_act, key_act, value_act, filter_taps, grad_out):
        count_all = query_act.shape[0] * query_act.shape[1]
        return jax.shard_map(
            functools.partial(shards, count_all=count_all),
            mesh=fine,
            in_specs=(spec, spec, spec, P(), spec),
            out_specs=(spec, spec, spec, P()),
            check_vma=False,
        )(query_act, key_act, value_act, filter_taps, grad_out)

    return whole
```

```python
import functools
import math

import jax
import jax.numpy as jnp
import ml_dtypes
import numpy as np
from jax import lax
from jax.experimental import pallas as pl
from jax.experimental.pallas import tpu as pltpu
from jax.sharding import Mesh, PartitionSpec as P

F32 = jnp.float32
BF16 = jnp.bfloat16
BLOCK = 128
SPEC = 256
HALF = BLOCK // 2
WIDTH = 256
VMEM_LIMIT = 40 * 1024 * 1024


def split_in_two(matrix):
    high = matrix.astype(ml_dtypes.bfloat16)
    low = (matrix - high.astype(np.float64)).astype(ml_dtypes.bfloat16)
    return high, low


def transform_matrices():
    freqs = np.concatenate([np.arange(0, BLOCK, 2), np.arange(1, BLOCK, 2)])
    angles = 2 * np.pi * freqs[:, None] * np.arange(BLOCK)[None, :] / SPEC
    real, imag = np.cos(angles), -np.sin(angles)
    imag[0] = np.cos(np.pi * np.arange(BLOCK))
    forward = np.concatenate([real, imag], axis=0)
    weight = np.full((SPEC,), 2.0 / SPEC)
    weight[0] = weight[BLOCK] = 1.0 / SPEC
    inverse = (forward * weight[:, None]).T
    return (
        np.concatenate(split_in_two(forward), axis=1),
        np.concatenate(split_in_two(inverse), axis=0),
    )


def dot(left, right):
    return jnp.dot(left, right, preferred_element_type=F32)


def spectrum(forward, block):
    both = dot(forward, jnp.concatenate([block, block], axis=0))
    return both[:BLOCK], both[BLOCK:]


def inverse_of(inverse, real, imag):
    both = jnp.concatenate([real, imag], axis=0)
    high = both.astype(BF16)
    low = (both - high.astype(F32)).astype(BF16)
    terms = dot(inverse, high)
    return terms[:BLOCK] + terms[BLOCK:] + dot(inverse[:BLOCK], low)


def beside(first, second):
    def joined(a, b):
        return jnp.concatenate([a[:HALF] + b[:HALF], a[HALF:] - b[HALF:]], axis=0)

    return joined(first[0], second[0]), joined(first[1], second[1])


def first_row(shape):
    return lax.broadcasted_iota(jnp.int32, shape, 0) == 0


def product(left, right):
    return (left.astype(F32) * right.astype(F32)).astype(BF16)


def rows(block):
    return pl.ds(block * BLOCK, BLOCK)


def correlation_terms(grad, gated):
    real = grad[0] * gated[0]
    imag = grad[1] * gated[1]
    cross = grad[1] * gated[0] - grad[0] * gated[1]
    return real, imag, cross


def correlation(inverse, terms):
    real, imag, cross = terms
    top = first_row(real.shape)
    return inverse_of(
        inverse, real + jnp.where(top, 0.0, imag), jnp.where(top, imag, cross)
    )


def inner_kernel(gated_ref, mix_ref, fwd_ref, inv_ref, out_ref):
    fwd, inv = fwd_ref[...], inv_ref[...]
    blocks = gated_ref.shape[0] // BLOCK
    for part in range(gated_ref.shape[1] // WIDTH):
        chans = pl.ds(part * WIDTH, WIDTH)
        terms = None
        before = None
        for n in range(blocks):
            gated = spectrum(fwd, gated_ref[rows(n), chans])
            grad = spectrum(fwd, mix_ref[rows(n), chans])
            window = gated if before is None else beside(gated, before)
            more = correlation_terms(grad, window)
            terms = more if terms is None else tuple(a + b for a, b in zip(terms, more))
            before = gated
        out_ref[:, chans] = correlation(inv, terms)


def outer_kernel(halo_ref, mix_ref, inner_ref, fwd_ref, inv_ref, out_ref):
    fwd, inv = fwd_ref[...], inv_ref[...]
    for part in range(halo_ref.shape[1] // WIDTH):
        chans = pl.ds(part * WIDTH, WIDTH)
        halo = spectrum(fwd, halo_ref[:, chans])
        zero = jnp.zeros_like(halo[0])
        window = beside((zero, zero), halo)
        grad = spectrum(fwd, mix_ref[:, chans])
        total = inner_ref[:, chans] + correlation(inv, correlation_terms(grad, window))
        for piece in range(WIDTH // 128):
            out_ref[rows(part * (WIDTH // 128) + piece), :] = total[
                :, piece * 128 : (piece + 1) * 128
            ].astype(BF16)


def conv_kernel(
    gated_ref, mix_ref, key_ref, value_ref, grad_ref, before_ref, after_ref, taps_ref, fwd_ref, inv_ref,
    out_query_ref, out_key_ref, out_value_ref,
):
    fwd, inv = fwd_ref[...], inv_ref[...]
    blocks = gated_ref.shape[0] // BLOCK
    real, imag = spectrum(fwd, taps_ref[...])
    top = first_row(real.shape)
    cross = jnp.where(top, 0.0, imag)
    last = jnp.where(top, imag, real)

    def backward(n, grad, after):
        wr, wi = beside(grad, after)
        carried = inverse_of(inv, wr * real + wi * cross, wi * last - wr * cross)
        out_key_ref[0, rows(n), :] = (carried * value_ref[0, rows(n), :].astype(F32)).astype(BF16)
        out_value_ref[0, rows(n), :] = (carried * key_ref[0, rows(n), :].astype(F32)).astype(BF16)

    before = spectrum(fwd, before_ref[...])
    earlier = None
    for n in range(blocks):
        gated = spectrum(fwd, gated_ref[rows(n), :])
        grad = spectrum(fwd, mix_ref[rows(n), :])
        wr, wi = beside(gated, before)
        mixed = inverse_of(inv, wr * real - wi * cross, wr * cross + wi * last)
        out_query_ref[0, rows(n), :] = (grad_ref[0, rows(n), :].astype(F32) * mixed).astype(BF16)
        if earlier is not None:
            backward(n - 1, earlier, grad)
        before, earlier = gated, grad
    backward(blocks - 1, earlier, spectrum(fwd, after_ref[...]))


def params():
    return pltpu.CompilerParams(vmem_limit_bytes=VMEM_LIMIT)


def cost(flops, moved):
    return pl.CostEstimate(flops=flops, bytes_accessed=moved, transcendentals=0)


def shards(query_act, key_act, value_act, filter_taps, grad_out, count_all=1):
    _, row_count, chan_count = query_act.shape
    blocks = row_count // BLOCK
    fwd_np, inv_np = transform_matrices()
    fwd, inv = jnp.asarray(fwd_np), jnp.asarray(inv_np)

    whole = pl.BlockSpec((1, row_count, chan_count), lambda i: (0, 0, 0))
    stack = pl.BlockSpec((row_count, chan_count), lambda i: (0, 0))
    slab = pl.BlockSpec((BLOCK, chan_count), lambda i: (0, 0))
    fwd_spec = pl.BlockSpec(fwd.shape, lambda i: (0, 0))
    inv_spec = pl.BlockSpec(inv.shape, lambda i: (0, 0))

    gated = product(key_act[0], value_act[0])
    mix = product(query_act[0], grad_out[0])

    ctx = ("z", "xh", "c")
    ring = 1
    for name in ctx:
        ring *= lax.axis_size(name)
    gated_edge, mix_edge = gated[row_count - BLOCK :], mix[:BLOCK]
    first_core = lax.axis_index("c") == 0
    inside = [(i, i + 1) for i in range(0, ring - 1, 2)]
    outside = [(i, i + 1) for i in range(1, ring - 1, 2)]
    both_ways = [pairs + [(j, i) for i, j in pairs] for pairs in (inside, outside)]
    from_inside = lax.ppermute(jnp.where(first_core, gated_edge, mix_edge), ctx, both_ways[0])
    to_outside = jnp.where(
        first_core,
        product(query_act[0, :BLOCK], grad_out[0, :BLOCK]),
        product(key_act[0, row_count - BLOCK :], value_act[0, row_count - BLOCK :]),
    )
    from_outside = lax.ppermute(to_outside, ctx, both_ways[1])
    before = jnp.where(first_core, from_outside, from_inside)
    after = jnp.where(first_core, from_inside, from_outside)

    close = pl.BlockSpec(memory_space=pltpu.VMEM)
    inner = pl.pallas_call(
        inner_kernel,
        in_specs=[close] * 4,
        out_specs=close,
        out_shape=jax.ShapeDtypeStruct((BLOCK, chan_count), F32),
        compiler_params=params(),
        cost_estimate=cost(800_000_000, 2_500_000),
        name="inner_pairs",
    )(gated, mix, fwd, inv)

    partial = pl.pallas_call(
        outer_kernel,
        in_specs=[close] * 5,
        out_specs=close,
        out_shape=jax.ShapeDtypeStruct((BLOCK * chan_count // 128, 128), BF16),
        compiler_params=params(),
        cost_estimate=cost(200_000_000, 800_000),
        name="outer_pairs",
    )(before, mix_edge, inner, fwd, inv)

    near = ("c", "xh", "xl", "y")
    near_count = 1
    for name in near:
        near_count *= lax.axis_size(name)
    far = "z"
    far_count = lax.axis_size(far)
    chunks = partial.reshape(near_count, -1, 128)
    mine = lax.all_to_all(chunks, near, 0, 0, tiled=True).astype(F32).sum(axis=0)
    out_shape = jax.ShapeDtypeStruct(query_act.shape, BF16)
    grad_query, grad_key, grad_value = pl.pallas_call(
        conv_kernel,
        grid=(1,),
        in_specs=[stack, stack, whole, whole, whole, slab, slab, slab, fwd_spec, inv_spec],
        out_specs=[whole, whole, whole],
        out_shape=[out_shape, out_shape, out_shape],
        compiler_params=params(),
        cost_estimate=cost(2_000_000_000, 4_000_000),
        name="convolutions",
    )(gated, mix, key_act, value_act, grad_out, before, after, filter_taps, fwd, inv)
    mine, grad_query, grad_key, grad_value = lax.optimization_barrier(
        (mine, grad_query, grad_key, grad_value)
    )
    planes = jnp.broadcast_to(mine.astype(BF16)[None], (far_count,) + mine.shape)
    mine = lax.all_to_all(planes, far, 0, 0, tiled=True).astype(F32).sum(axis=0) / math.sqrt(count_all)
    copies = jnp.broadcast_to(mine.astype(BF16)[None], (near_count,) + mine.shape)
    total = lax.all_to_all(copies, near, 0, 0, tiled=True)
    total = total.reshape(chan_count // 128, BLOCK, 128).astype(F32)
    grad_filter = jnp.concatenate([total[i] for i in range(chan_count // 128)], axis=1)

    return grad_query, grad_key, grad_value, grad_filter


def solution(mesh):
    fine = Mesh(mesh.devices.reshape(8, 2, 2, 4, 2), ("z", "xh", "c", "y", "xl"))
    spec = P(("y", "xl"), ("z", "xh", "c"), None)

    def whole(query_act, key_act, value_act, filter_taps, grad_out):
        count_all = query_act.shape[0] * query_act.shape[1]
        return jax.shard_map(
            functools.partial(shards, count_all=count_all),
            mesh=fine,
            in_specs=(spec, spec, spec, P(), spec),
            out_specs=(spec, spec, spec, P()),
            check_vma=False,
        )(query_act, key_act, value_act, filter_taps, grad_out)

    return whole
```

```python
import functools
import math

import jax
import jax.numpy as jnp
import ml_dtypes
import numpy as np
from jax import lax
from jax.experimental import pallas as pl
from jax.experimental.pallas import tpu as pltpu
from jax.sharding import Mesh, PartitionSpec as P

F32 = jnp.float32
BF16 = jnp.bfloat16
BLOCK = 128
SPEC = 256
HALF = BLOCK // 2
WIDTH = 256
VMEM_LIMIT = 40 * 1024 * 1024


def split_in_two(matrix):
    high = matrix.astype(ml_dtypes.bfloat16)
    low = (matrix - high.astype(np.float64)).astype(ml_dtypes.bfloat16)
    return high, low


def transform_matrices():
    freqs = np.concatenate([np.arange(0, BLOCK, 2), np.arange(1, BLOCK, 2)])
    angles = 2 * np.pi * freqs[:, None] * np.arange(BLOCK)[None, :] / SPEC
    real, imag = np.cos(angles), -np.sin(angles)
    imag[0] = np.cos(np.pi * np.arange(BLOCK))
    forward = np.concatenate([real, imag], axis=0)
    weight = np.full((SPEC,), 2.0 / SPEC)
    weight[0] = weight[BLOCK] = 1.0 / SPEC
    inverse = (forward * weight[:, None]).T
    return (
        np.concatenate(split_in_two(forward), axis=1),
        np.concatenate(split_in_two(inverse), axis=0),
    )


def dot(left, right):
    return jnp.dot(left, right, preferred_element_type=F32)


def spectrum(forward, block):
    both = dot(forward, jnp.concatenate([block, block], axis=0))
    return both[:BLOCK], both[BLOCK:]


def inverse_of(inverse, real, imag):
    both = jnp.concatenate([real, imag], axis=0)
    high = both.astype(BF16)
    low = (both - high.astype(F32)).astype(BF16)
    terms = dot(inverse, high)
    return terms[:BLOCK] + terms[BLOCK:] + dot(inverse[:BLOCK], low)


def beside(first, second):
    def joined(a, b):
        return jnp.concatenate([a[:HALF] + b[:HALF], a[HALF:] - b[HALF:]], axis=0)

    return joined(first[0], second[0]), joined(first[1], second[1])


def first_row(shape):
    return lax.broadcasted_iota(jnp.int32, shape, 0) == 0


def product(left, right):
    return (left.astype(F32) * right.astype(F32)).astype(BF16)


def rows(block):
    return pl.ds(block * BLOCK, BLOCK)


def correlation_terms(grad, gated):
    real = grad[0] * gated[0]
    imag = grad[1] * gated[1]
    cross = grad[1] * gated[0] - grad[0] * gated[1]
    return real, imag, cross


def correlation(inverse, terms):
    real, imag, cross = terms
    top = first_row(real.shape)
    return inverse_of(
        inverse, real + jnp.where(top, 0.0, imag), jnp.where(top, imag, cross)
    )


def inner_kernel(gated_ref, mix_ref, fwd_ref, inv_ref, out_ref):
    fwd, inv = fwd_ref[...], inv_ref[...]
    blocks = gated_ref.shape[0] // BLOCK
    for part in range(gated_ref.shape[1] // WIDTH):
        chans = pl.ds(part * WIDTH, WIDTH)
        terms = None
        before = None
        for n in range(blocks):
            gated = spectrum(fwd, gated_ref[rows(n), chans])
            grad = spectrum(fwd, mix_ref[rows(n), chans])
            window = gated if before is None else beside(gated, before)
            more = correlation_terms(grad, window)
            terms = more if terms is None else tuple(a + b for a, b in zip(terms, more))
            before = gated
        out_ref[:, chans] = correlation(inv, terms)


def outer_kernel(halo_ref, mix_ref, inner_ref, fwd_ref, inv_ref, out_ref):
    fwd, inv = fwd_ref[...], inv_ref[...]
    for part in range(halo_ref.shape[1] // WIDTH):
        chans = pl.ds(part * WIDTH, WIDTH)
        halo = spectrum(fwd, halo_ref[:, chans])
        zero = jnp.zeros_like(halo[0])
        window = beside((zero, zero), halo)
        grad = spectrum(fwd, mix_ref[:, chans])
        total = inner_ref[:, chans] + correlation(inv, correlation_terms(grad, window))
        for piece in range(WIDTH // 128):
            out_ref[rows(part * (WIDTH // 128) + piece), :] = total[
                :, piece * 128 : (piece + 1) * 128
            ].astype(BF16)


def conv_kernel(
    gated_ref, mix_ref, key_ref, value_ref, grad_ref, before_ref, after_ref, taps_ref, fwd_ref, inv_ref,
    out_query_ref, out_key_ref, out_value_ref,
):
    fwd, inv = fwd_ref[...], inv_ref[...]
    blocks = gated_ref.shape[0] // BLOCK
    real, imag = spectrum(fwd, taps_ref[...])
    top = first_row(real.shape)
    cross = jnp.where(top, 0.0, imag)
    last = jnp.where(top, imag, real)

    def backward(n, grad, after):
        wr, wi = beside(grad, after)
        carried = inverse_of(inv, wr * real + wi * cross, wi * last - wr * cross)
        out_key_ref[0, rows(n), :] = (carried * value_ref[0, rows(n), :].astype(F32)).astype(BF16)
        out_value_ref[0, rows(n), :] = (carried * key_ref[0, rows(n), :].astype(F32)).astype(BF16)

    before = spectrum(fwd, before_ref[...])
    earlier = None
    for n in range(blocks):
        gated = spectrum(fwd, gated_ref[rows(n), :])
        grad = spectrum(fwd, mix_ref[rows(n), :])
        wr, wi = beside(gated, before)
        mixed = inverse_of(inv, wr * real - wi * cross, wr * cross + wi * last)
        out_query_ref[0, rows(n), :] = (grad_ref[0, rows(n), :].astype(F32) * mixed).astype(BF16)
        if earlier is not None:
            backward(n - 1, earlier, grad)
        before, earlier = gated, grad
    backward(blocks - 1, earlier, spectrum(fwd, after_ref[...]))


def params():
    return pltpu.CompilerParams(vmem_limit_bytes=VMEM_LIMIT)


def cost(flops, moved):
    return pl.CostEstimate(flops=flops, bytes_accessed=moved, transcendentals=0)


def shards(query_act, key_act, value_act, filter_taps, grad_out, count_all=1):
    _, row_count, chan_count = query_act.shape
    blocks = row_count // BLOCK
    fwd_np, inv_np = transform_matrices()
    fwd, inv = jnp.asarray(fwd_np), jnp.asarray(inv_np)

    whole = pl.BlockSpec((1, row_count, chan_count), lambda i: (0, 0, 0))
    stack = pl.BlockSpec((row_count, chan_count), lambda i: (0, 0))
    slab = pl.BlockSpec((BLOCK, chan_count), lambda i: (0, 0))
    fwd_spec = pl.BlockSpec(fwd.shape, lambda i: (0, 0))
    inv_spec = pl.BlockSpec(inv.shape, lambda i: (0, 0))

    gated = product(key_act[0], value_act[0])
    mix = product(query_act[0], grad_out[0])

    ctx = ("z", "xh", "c")
    ring = 1
    for name in ctx:
        ring *= lax.axis_size(name)
    gated_edge, mix_edge = gated[row_count - BLOCK :], mix[:BLOCK]
    first_core = lax.axis_index("c") == 0
    inside = [(i, i + 1) for i in range(0, ring - 1, 2)]
    outside = [(i, i + 1) for i in range(1, ring - 1, 2)]
    both_ways = [pairs + [(j, i) for i, j in pairs] for pairs in (inside, outside)]
    from_inside = lax.ppermute(jnp.where(first_core, gated_edge, mix_edge), ctx, both_ways[0])
    to_outside = jnp.where(
        first_core,
        product(query_act[0, :BLOCK], grad_out[0, :BLOCK]),
        product(key_act[0, row_count - BLOCK :], value_act[0, row_count - BLOCK :]),
    )
    from_outside = lax.ppermute(to_outside, ctx, both_ways[1])
    before = jnp.where(first_core, from_outside, from_inside)
    after = jnp.where(first_core, from_inside, from_outside)

    close = pl.BlockSpec(memory_space=pltpu.VMEM)
    inner = pl.pallas_call(
        inner_kernel,
        in_specs=[close] * 4,
        out_specs=close,
        out_shape=jax.ShapeDtypeStruct((BLOCK, chan_count), F32),
        compiler_params=params(),
        cost_estimate=cost(800_000_000, 2_500_000),
        name="inner_pairs",
    )(gated, mix, fwd, inv)

    partial = pl.pallas_call(
        outer_kernel,
        in_specs=[close] * 5,
        out_specs=close,
        out_shape=jax.ShapeDtypeStruct((BLOCK * chan_count // 128, 128), BF16),
        compiler_params=params(),
        cost_estimate=cost(200_000_000, 800_000),
        name="outer_pairs",
    )(before, mix_edge, inner, fwd, inv)

    near = ("c", "xh", "xl", "y")
    near_count = 1
    for name in near:
        near_count *= lax.axis_size(name)
    far = "z"
    far_count = lax.axis_size(far)
    chunks = partial.reshape(near_count, -1, 128)
    mine = lax.all_to_all(chunks, near, 0, 0, tiled=True).astype(F32).sum(axis=0)
    mine, before, after = lax.optimization_barrier((mine, before, after))
    out_shape = jax.ShapeDtypeStruct(query_act.shape, BF16)
    grad_query, grad_key, grad_value = pl.pallas_call(
        conv_kernel,
        grid=(1,),
        in_specs=[stack, stack, whole, whole, whole, slab, slab, slab, fwd_spec, inv_spec],
        out_specs=[whole, whole, whole],
        out_shape=[out_shape, out_shape, out_shape],
        compiler_params=params(),
        cost_estimate=cost(2_000_000_000, 4_000_000),
        name="convolutions",
    )(gated, mix, key_act, value_act, grad_out, before, after, filter_taps, fwd, inv)
    planes = jnp.broadcast_to(mine.astype(BF16)[None], (far_count,) + mine.shape)
    mine = lax.all_to_all(planes, far, 0, 0, tiled=True).astype(F32).sum(axis=0) / math.sqrt(count_all)
    mine, grad_query, grad_key, grad_value = lax.optimization_barrier(
        (mine, grad_query, grad_key, grad_value)
    )
    copies = jnp.broadcast_to(mine.astype(BF16)[None], (near_count,) + mine.shape)
    total = lax.all_to_all(copies, near, 0, 0, tiled=True)
    total = total.reshape(chan_count // 128, BLOCK, 128).astype(F32)
    grad_filter = jnp.concatenate([total[i] for i in range(chan_count // 128)], axis=1)

    return grad_query, grad_key, grad_value, grad_filter


def solution(mesh):
    fine = Mesh(mesh.devices.reshape(8, 2, 2, 4, 2), ("z", "xh", "c", "y", "xl"))
    spec = P(("y", "xl"), ("z", "xh", "c"), None)

    def whole(query_act, key_act, value_act, filter_taps, grad_out):
        count_all = query_act.shape[0] * query_act.shape[1]
        return jax.shard_map(
            functools.partial(shards, count_all=count_all),
            mesh=fine,
            in_specs=(spec, spec, spec, P(), spec),
            out_specs=(spec, spec, spec, P()),
            check_vma=False,
        )(query_act, key_act, value_act, filter_taps, grad_out)

    return whole
```

```python
import functools
import math

import jax
import jax.numpy as jnp
import ml_dtypes
import numpy as np
from jax import lax
from jax.experimental import pallas as pl
from jax.experimental.pallas import tpu as pltpu
from jax.sharding import Mesh, PartitionSpec as P

F32 = jnp.float32
BF16 = jnp.bfloat16
BLOCK = 128
SPEC = 256
HALF = BLOCK // 2
WIDTH = 512
VMEM_LIMIT = 40 * 1024 * 1024


def split_in_two(matrix):
    high = matrix.astype(ml_dtypes.bfloat16)
    low = (matrix - high.astype(np.float64)).astype(ml_dtypes.bfloat16)
    return high, low


def transform_matrices():
    freqs = np.concatenate([np.arange(0, BLOCK, 2), np.arange(1, BLOCK, 2)])
    angles = 2 * np.pi * freqs[:, None] * np.arange(BLOCK)[None, :] / SPEC
    real, imag = np.cos(angles), -np.sin(angles)
    imag[0] = np.cos(np.pi * np.arange(BLOCK))
    forward = np.concatenate([real, imag], axis=0)
    weight = np.full((SPEC,), 2.0 / SPEC)
    weight[0] = weight[BLOCK] = 1.0 / SPEC
    inverse = (forward * weight[:, None]).T
    return (
        np.concatenate(split_in_two(forward), axis=1),
        np.concatenate(split_in_two(inverse), axis=0),
    )


def dot(left, right):
    return jnp.dot(left, right, preferred_element_type=F32)


def spectrum(forward, block):
    both = dot(forward, jnp.concatenate([block, block], axis=0))
    return both[:BLOCK], both[BLOCK:]


def inverse_of(inverse, real, imag):
    both = jnp.concatenate([real, imag], axis=0)
    high = both.astype(BF16)
    low = (both - high.astype(F32)).astype(BF16)
    terms = dot(inverse, high)
    return terms[:BLOCK] + terms[BLOCK:] + dot(inverse[:BLOCK], low)


def beside(first, second):
    def joined(a, b):
        return jnp.concatenate([a[:HALF] + b[:HALF], a[HALF:] - b[HALF:]], axis=0)

    return joined(first[0], second[0]), joined(first[1], second[1])


def first_row(shape):
    return lax.broadcasted_iota(jnp.int32, shape, 0) == 0


def product(left, right):
    return (left.astype(F32) * right.astype(F32)).astype(BF16)


def rows(block):
    return pl.ds(block * BLOCK, BLOCK)


def correlation_terms(grad, gated):
    real = grad[0] * gated[0]
    imag = grad[1] * gated[1]
    cross = grad[1] * gated[0] - grad[0] * gated[1]
    return real, imag, cross


def correlation(inverse, terms):
    real, imag, cross = terms
    top = first_row(real.shape)
    return inverse_of(
        inverse, real + jnp.where(top, 0.0, imag), jnp.where(top, imag, cross)
    )


def inner_kernel(gated_ref, mix_ref, fwd_ref, inv_ref, out_ref, edge_ref):
    fwd, inv = fwd_ref[...], inv_ref[...]
    blocks = gated_ref.shape[0] // BLOCK
    for part in range(gated_ref.shape[1] // WIDTH):
        chans = pl.ds(part * WIDTH, WIDTH)
        terms = None
        before = None
        for n in range(blocks):
            gated = spectrum(fwd, gated_ref[rows(n), chans])
            grad = spectrum(fwd, mix_ref[rows(n), chans])
            if n == 0:
                edge_ref[:BLOCK, chans], edge_ref[BLOCK:, chans] = grad
            window = gated if before is None else beside(gated, before)
            more = correlation_terms(grad, window)
            terms = more if terms is None else tuple(a + b for a, b in zip(terms, more))
            before = gated
        out_ref[:, chans] = correlation(inv, terms)


def outer_kernel(halo_ref, edge_ref, inner_ref, fwd_ref, inv_ref, out_ref):
    fwd, inv = fwd_ref[...], inv_ref[...]
    for part in range(halo_ref.shape[1] // WIDTH):
        chans = pl.ds(part * WIDTH, WIDTH)
        halo = spectrum(fwd, halo_ref[:, chans])
        zero = jnp.zeros_like(halo[0])
        window = beside((zero, zero), halo)
        grad = edge_ref[:BLOCK, chans], edge_ref[BLOCK:, chans]
        total = inner_ref[:, chans] + correlation(inv, correlation_terms(grad, window))
        for piece in range(WIDTH // 128):
            out_ref[rows(part * (WIDTH // 128) + piece), :] = total[
                :, piece * 128 : (piece + 1) * 128
            ].astype(BF16)


def conv_kernel(
    gated_ref, mix_ref, key_ref, value_ref, grad_ref, before_ref, after_ref, taps_ref, fwd_ref, inv_ref,
    out_query_ref, out_key_ref, out_value_ref,
):
    fwd, inv = fwd_ref[...], inv_ref[...]
    blocks = gated_ref.shape[0] // BLOCK
    real, imag = spectrum(fwd, taps_ref[...])
    top = first_row(real.shape)
    cross = jnp.where(top, 0.0, imag)
    last = jnp.where(top, imag, real)

    def backward(n, grad, after):
        wr, wi = beside(grad, after)
        carried = inverse_of(inv, wr * real + wi * cross, wi * last - wr * cross)
        out_key_ref[0, rows(n), :] = (carried * value_ref[0, rows(n), :].astype(F32)).astype(BF16)
        out_value_ref[0, rows(n), :] = (carried * key_ref[0, rows(n), :].astype(F32)).astype(BF16)

    before = spectrum(fwd, before_ref[...])
    earlier = None
    for n in range(blocks):
        gated = spectrum(fwd, gated_ref[rows(n), :])
        grad = spectrum(fwd, mix_ref[rows(n), :])
        wr, wi = beside(gated, before)
        mixed = inverse_of(inv, wr * real - wi * cross, wr * cross + wi * last)
        out_query_ref[0, rows(n), :] = (grad_ref[0, rows(n), :].astype(F32) * mixed).astype(BF16)
        if earlier is not None:
            backward(n - 1, earlier, grad)
        before, earlier = gated, grad
    backward(blocks - 1, earlier, spectrum(fwd, after_ref[...]))


def params():
    return pltpu.CompilerParams(vmem_limit_bytes=VMEM_LIMIT)


def cost(flops, moved):
    return pl.CostEstimate(flops=flops, bytes_accessed=moved, transcendentals=0)


def shards(query_act, key_act, value_act, filter_taps, grad_out, count_all=1):
    _, row_count, chan_count = query_act.shape
    blocks = row_count // BLOCK
    fwd_np, inv_np = transform_matrices()
    fwd, inv = jnp.asarray(fwd_np), jnp.asarray(inv_np)

    whole = pl.BlockSpec((1, row_count, chan_count), lambda i: (0, 0, 0))
    stack = pl.BlockSpec((row_count, chan_count), lambda i: (0, 0))
    slab = pl.BlockSpec((BLOCK, chan_count), lambda i: (0, 0))
    fwd_spec = pl.BlockSpec(fwd.shape, lambda i: (0, 0))
    inv_spec = pl.BlockSpec(inv.shape, lambda i: (0, 0))

    gated = product(key_act[0], value_act[0])
    mix = product(query_act[0], grad_out[0])

    ctx = ("z", "xh", "c")
    ring = 1
    for name in ctx:
        ring *= lax.axis_size(name)
    gated_edge, mix_edge = gated[row_count - BLOCK :], mix[:BLOCK]
    first_core = lax.axis_index("c") == 0
    inside = [(i, i + 1) for i in range(0, ring - 1, 2)]
    outside = [(i, i + 1) for i in range(1, ring - 1, 2)]
    both_ways = [pairs + [(j, i) for i, j in pairs] for pairs in (inside, outside)]
    from_inside = lax.ppermute(jnp.where(first_core, gated_edge, mix_edge), ctx, both_ways[0])
    to_outside = jnp.where(
        first_core,
        product(query_act[0, :BLOCK], grad_out[0, :BLOCK]),
        product(key_act[0, row_count - BLOCK :], value_act[0, row_count - BLOCK :]),
    )
    from_outside = lax.ppermute(to_outside, ctx, both_ways[1])
    before = jnp.where(first_core, from_outside, from_inside)
    after = jnp.where(first_core, from_inside, from_outside)

    close = pl.BlockSpec(memory_space=pltpu.VMEM)
    inner, edge_spectrum = pl.pallas_call(
        inner_kernel,
        in_specs=[close] * 4,
        out_specs=[close] * 2,
        out_shape=[
            jax.ShapeDtypeStruct((BLOCK, chan_count), F32),
            jax.ShapeDtypeStruct((SPEC, chan_count), F32),
        ],
        compiler_params=params(),
        cost_estimate=cost(800_000_000, 2_500_000),
        name="inner_pairs",
    )(gated, mix, fwd, inv)

    partial = pl.pallas_call(
        outer_kernel,
        in_specs=[close] * 5,
        out_specs=close,
        out_shape=jax.ShapeDtypeStruct((BLOCK * chan_count // 128, 128), BF16),
        compiler_params=params(),
        cost_estimate=cost(200_000_000, 800_000),
        name="outer_pairs",
    )(before, edge_spectrum, inner, fwd, inv)

    near = ("c", "xh", "xl", "y")
    near_count = 1
    for name in near:
        near_count *= lax.axis_size(name)
    far = "z"
    far_count = lax.axis_size(far)
    chunks = partial.reshape(near_count, -1, 128)
    mine = lax.all_to_all(chunks, near, 0, 0, tiled=True).astype(F32).sum(axis=0)
    mine, before, after = lax.optimization_barrier((mine, before, after))
    out_shape = jax.ShapeDtypeStruct(query_act.shape, BF16)
    grad_query, grad_key, grad_value = pl.pallas_call(
        conv_kernel,
        grid=(1,),
        in_specs=[stack, stack, whole, whole, whole, slab, slab, slab, fwd_spec, inv_spec],
        out_specs=[whole, whole, whole],
        out_shape=[out_shape, out_shape, out_shape],
        compiler_params=params(),
        cost_estimate=cost(2_000_000_000, 4_000_000),
        name="convolutions",
    )(gated, mix, key_act, value_act, grad_out, before, after, filter_taps, fwd, inv)
    planes = jnp.broadcast_to(mine.astype(BF16)[None], (far_count,) + mine.shape)
    mine = lax.all_to_all(planes, far, 0, 0, tiled=True).astype(F32).sum(axis=0) / math.sqrt(count_all)
    mine, grad_query, grad_key, grad_value = lax.optimization_barrier(
        (mine, grad_query, grad_key, grad_value)
    )
    copies = jnp.broadcast_to(mine.astype(BF16)[None], (near_count,) + mine.shape)
    total = lax.all_to_all(copies, near, 0, 0, tiled=True)
    total = total.reshape(chan_count // 128, BLOCK, 128).astype(F32)
    grad_filter = jnp.concatenate([total[i] for i in range(chan_count // 128)], axis=1)

    return grad_query, grad_key, grad_value, grad_filter


def solution(mesh):
    fine = Mesh(mesh.devices.reshape(8, 2, 2, 4, 2), ("z", "xh", "c", "y", "xl"))
    spec = P(("y", "xl"), ("z", "xh", "c"), None)

    def whole(query_act, key_act, value_act, filter_taps, grad_out):
        count_all = query_act.shape[0] * query_act.shape[1]
        return jax.shard_map(
            functools.partial(shards, count_all=count_all),
            mesh=fine,
            in_specs=(spec, spec, spec, P(), spec),
            out_specs=(spec, spec, spec, P()),
            check_vma=False,
        )(query_act, key_act, value_act, filter_taps, grad_out)

    return whole
```

```python
import functools
import math

import jax
import jax.numpy as jnp
import ml_dtypes
import numpy as np
from jax import lax
from jax.experimental import pallas as pl
from jax.experimental.pallas import tpu as pltpu
from jax.sharding import Mesh, PartitionSpec as P

F32 = jnp.float32
BF16 = jnp.bfloat16
BLOCK = 128
SPEC = 256
HALF = BLOCK // 2
WIDTH = 512
VMEM_LIMIT = 40 * 1024 * 1024


def split_in_two(matrix):
    high = matrix.astype(ml_dtypes.bfloat16)
    low = (matrix - high.astype(np.float64)).astype(ml_dtypes.bfloat16)
    return high, low


def transform_matrices():
    freqs = np.concatenate([np.arange(0, BLOCK, 2), np.arange(1, BLOCK, 2)])
    angles = 2 * np.pi * freqs[:, None] * np.arange(BLOCK)[None, :] / SPEC
    real, imag = np.cos(angles), -np.sin(angles)
    imag[0] = np.cos(np.pi * np.arange(BLOCK))
    forward = np.concatenate([real, imag], axis=0)
    weight = np.full((SPEC,), 2.0 / SPEC)
    weight[0] = weight[BLOCK] = 1.0 / SPEC
    inverse = (forward * weight[:, None]).T
    return (
        np.concatenate(split_in_two(forward), axis=1),
        np.concatenate(split_in_two(inverse), axis=0),
    )


def dot(left, right):
    return jnp.dot(left, right, preferred_element_type=F32)


def spectrum(forward, block):
    both = dot(forward, jnp.concatenate([block, block], axis=0))
    return both[:BLOCK], both[BLOCK:]


def inverse_of(inverse, real, imag):
    both = jnp.concatenate([real, imag], axis=0)
    high = both.astype(BF16)
    low = (both - high.astype(F32)).astype(BF16)
    terms = dot(inverse, high)
    return terms[:BLOCK] + terms[BLOCK:] + dot(inverse[:BLOCK], low)


def beside(first, second):
    def joined(a, b):
        return jnp.concatenate([a[:HALF] + b[:HALF], a[HALF:] - b[HALF:]], axis=0)

    return joined(first[0], second[0]), joined(first[1], second[1])


def first_row(shape):
    return lax.broadcasted_iota(jnp.int32, shape, 0) == 0


def product(left, right):
    return (left.astype(F32) * right.astype(F32)).astype(BF16)


def rows(block):
    return pl.ds(block * BLOCK, BLOCK)


def correlation_terms(grad, gated):
    real = grad[0] * gated[0]
    imag = grad[1] * gated[1]
    cross = grad[1] * gated[0] - grad[0] * gated[1]
    return real, imag, cross


def correlation(inverse, terms):
    real, imag, cross = terms
    top = first_row(real.shape)
    return inverse_of(
        inverse, real + jnp.where(top, 0.0, imag), jnp.where(top, imag, cross)
    )


def inner_kernel(gated_ref, mix_ref, fwd_ref, inv_ref, out_ref, edge_ref):
    fwd, inv = fwd_ref[...], inv_ref[...]
    blocks = gated_ref.shape[0] // BLOCK
    for part in range(gated_ref.shape[1] // WIDTH):
        chans = pl.ds(part * WIDTH, WIDTH)
        terms = None
        before = None
        for n in range(blocks):
            gated = spectrum(fwd, gated_ref[rows(n), chans])
            grad = spectrum(fwd, mix_ref[rows(n), chans])
            if n == 0:
                edge_ref[:BLOCK, chans], edge_ref[BLOCK:, chans] = grad
            window = gated if before is None else beside(gated, before)
            more = correlation_terms(grad, window)
            terms = more if terms is None else tuple(a + b for a, b in zip(terms, more))
            before = gated
        out_ref[:, chans] = correlation(inv, terms)


def outer_kernel(halo_ref, edge_ref, inner_ref, fwd_ref, inv_ref, out_ref):
    fwd, inv = fwd_ref[...], inv_ref[...]
    for part in range(halo_ref.shape[1] // WIDTH):
        chans = pl.ds(part * WIDTH, WIDTH)
        halo = spectrum(fwd, halo_ref[:, chans])
        zero = jnp.zeros_like(halo[0])
        window = beside((zero, zero), halo)
        grad = edge_ref[:BLOCK, chans], edge_ref[BLOCK:, chans]
        total = inner_ref[:, chans] + correlation(inv, correlation_terms(grad, window))
        for piece in range(WIDTH // 128):
            out_ref[rows(part * (WIDTH // 128) + piece), :] = total[
                :, piece * 128 : (piece + 1) * 128
            ].astype(BF16)


def conv_kernel(
    gated_ref, mix_ref, key_ref, value_ref, grad_ref, before_ref, after_ref, taps_ref, fwd_ref, inv_ref,
    out_query_ref, out_key_ref, out_value_ref,
):
    fwd, inv = fwd_ref[...], inv_ref[...]
    blocks = gated_ref.shape[0] // BLOCK
    real, imag = spectrum(fwd, taps_ref[...])
    top = first_row(real.shape)
    cross = jnp.where(top, 0.0, imag)
    last = jnp.where(top, imag, real)

    def backward(n, grad, after):
        wr, wi = beside(grad, after)
        carried = inverse_of(inv, wr * real + wi * cross, wi * last - wr * cross)
        out_key_ref[0, rows(n), :] = (carried * value_ref[0, rows(n), :].astype(F32)).astype(BF16)
        out_value_ref[0, rows(n), :] = (carried * key_ref[0, rows(n), :].astype(F32)).astype(BF16)

    before = spectrum(fwd, before_ref[...])
    earlier = None
    for n in range(blocks):
        gated = spectrum(fwd, gated_ref[rows(n), :])
        grad = spectrum(fwd, mix_ref[rows(n), :])
        wr, wi = beside(gated, before)
        mixed = inverse_of(inv, wr * real - wi * cross, wr * cross + wi * last)
        out_query_ref[0, rows(n), :] = (grad_ref[0, rows(n), :].astype(F32) * mixed).astype(BF16)
        if earlier is not None:
            backward(n - 1, earlier, grad)
        before, earlier = gated, grad
    backward(blocks - 1, earlier, spectrum(fwd, after_ref[...]))


def spread_kernel(terms_ref, out_ref):
    total = jnp.sum(terms_ref[...].astype(F32), axis=0).astype(BF16)
    for place in range(out_ref.shape[0]):
        out_ref[place] = total


def params():
    return pltpu.CompilerParams(vmem_limit_bytes=VMEM_LIMIT)


def cost(flops, moved):
    return pl.CostEstimate(flops=flops, bytes_accessed=moved, transcendentals=0)


def shards(query_act, key_act, value_act, filter_taps, grad_out, count_all=1):
    _, row_count, chan_count = query_act.shape
    blocks = row_count // BLOCK
    fwd_np, inv_np = transform_matrices()
    fwd, inv = jnp.asarray(fwd_np), jnp.asarray(inv_np)

    whole = pl.BlockSpec((1, row_count, chan_count), lambda i: (0, 0, 0))
    stack = pl.BlockSpec((row_count, chan_count), lambda i: (0, 0))
    slab = pl.BlockSpec((BLOCK, chan_count), lambda i: (0, 0))
    fwd_spec = pl.BlockSpec(fwd.shape, lambda i: (0, 0))
    inv_spec = pl.BlockSpec(inv.shape, lambda i: (0, 0))

    gated = product(key_act[0], value_act[0])
    mix = product(query_act[0], grad_out[0])

    ctx = ("z", "xh", "c")
    ring = 1
    for name in ctx:
        ring *= lax.axis_size(name)
    gated_edge, mix_edge = gated[row_count - BLOCK :], mix[:BLOCK]
    first_core = lax.axis_index("c") == 0
    inside = [(i, i + 1) for i in range(0, ring - 1, 2)]
    outside = [(i, i + 1) for i in range(1, ring - 1, 2)]
    both_ways = [pairs + [(j, i) for i, j in pairs] for pairs in (inside, outside)]
    from_inside = lax.ppermute(jnp.where(first_core, gated_edge, mix_edge), ctx, both_ways[0])
    to_outside = jnp.where(
        first_core,
        product(query_act[0, :BLOCK], grad_out[0, :BLOCK]),
        product(key_act[0, row_count - BLOCK :], value_act[0, row_count - BLOCK :]),
    )
    from_outside = lax.ppermute(to_outside, ctx, both_ways[1])
    before = jnp.where(first_core, from_outside, from_inside)
    after = jnp.where(first_core, from_inside, from_outside)

    close = pl.BlockSpec(memory_space=pltpu.VMEM)
    inner, edge_spectrum = pl.pallas_call(
        inner_kernel,
        in_specs=[close] * 4,
        out_specs=[close] * 2,
        out_shape=[
            jax.ShapeDtypeStruct((BLOCK, chan_count), F32),
            jax.ShapeDtypeStruct((SPEC, chan_count), F32),
        ],
        compiler_params=params(),
        cost_estimate=cost(800_000_000, 2_500_000),
        name="inner_pairs",
    )(gated, mix, fwd, inv)

    partial = pl.pallas_call(
        outer_kernel,
        in_specs=[close] * 5,
        out_specs=close,
        out_shape=jax.ShapeDtypeStruct((BLOCK * chan_count // 128, 128), BF16),
        compiler_params=params(),
        cost_estimate=cost(200_000_000, 800_000),
        name="outer_pairs",
    )(before, edge_spectrum, inner, fwd, inv)

    near = ("c", "y", "xh", "xl")
    near_count = 1
    for name in near:
        near_count *= lax.axis_size(name)
    far = "z"
    far_count = lax.axis_size(far)
    chunks = partial.reshape(near_count, -1, 128)
    mine = lax.all_to_all(chunks, near, 0, 0, tiled=True)
    mine, before, after = lax.optimization_barrier((mine, before, after))
    out_shape = jax.ShapeDtypeStruct(query_act.shape, BF16)
    grad_query, grad_key, grad_value = pl.pallas_call(
        conv_kernel,
        grid=(1,),
        in_specs=[stack, stack, whole, whole, whole, slab, slab, slab, fwd_spec, inv_spec],
        out_specs=[whole, whole, whole],
        out_shape=[out_shape, out_shape, out_shape],
        compiler_params=params(),
        cost_estimate=cost(2_000_000_000, 4_000_000),
        name="convolutions",
    )(gated, mix, key_act, value_act, grad_out, before, after, filter_taps, fwd, inv)
    planes = pl.pallas_call(
        spread_kernel,
        in_specs=[close],
        out_specs=close,
        out_shape=jax.ShapeDtypeStruct((far_count,) + mine.shape[1:], BF16),
        compiler_params=params(),
        cost_estimate=cost(100_000, 200_000),
        name="spread",
    )(mine)
    mine = lax.all_to_all(planes, far, 0, 0, tiled=True).astype(F32).sum(axis=0) / math.sqrt(count_all)
    mine, grad_query, grad_key, grad_value = lax.optimization_barrier(
        (mine, grad_query, grad_key, grad_value)
    )
    copies = jnp.broadcast_to(mine.astype(BF16)[None], (near_count,) + mine.shape)
    total = lax.all_to_all(copies, near, 0, 0, tiled=True)
    total = total.reshape(chan_count // 128, BLOCK, 128).astype(F32)
    grad_filter = jnp.concatenate([total[i] for i in range(chan_count // 128)], axis=1)

    return grad_query, grad_key, grad_value, grad_filter


def solution(mesh):
    fine = Mesh(mesh.devices.reshape(8, 2, 2, 4, 2), ("z", "xh", "c", "y", "xl"))
    spec = P(("y", "xl"), ("z", "xh", "c"), None)

    def whole(query_act, key_act, value_act, filter_taps, grad_out):
        count_all = query_act.shape[0] * query_act.shape[1]
        return jax.shard_map(
            functools.partial(shards, count_all=count_all),
            mesh=fine,
            in_specs=(spec, spec, spec, P(), spec),
            out_specs=(spec, spec, spec, P()),
            check_vma=False,
        )(query_act, key_act, value_act, filter_taps, grad_out)

    return whole
```

```python
import functools
import math

import jax
import jax.numpy as jnp
import ml_dtypes
import numpy as np
from jax import lax
from jax.experimental import pallas as pl
from jax.experimental.pallas import tpu as pltpu
from jax.sharding import Mesh, PartitionSpec as P

F32 = jnp.float32
BF16 = jnp.bfloat16
BLOCK = 128
SPEC = 256
HALF = BLOCK // 2
WIDTH = 512
VMEM_LIMIT = 40 * 1024 * 1024


def split_in_two(matrix):
    high = matrix.astype(ml_dtypes.bfloat16)
    low = (matrix - high.astype(np.float64)).astype(ml_dtypes.bfloat16)
    return high, low


def transform_matrices():
    freqs = np.concatenate([np.arange(0, BLOCK, 2), np.arange(1, BLOCK, 2)])
    angles = 2 * np.pi * freqs[:, None] * np.arange(BLOCK)[None, :] / SPEC
    real, imag = np.cos(angles), -np.sin(angles)
    imag[0] = np.cos(np.pi * np.arange(BLOCK))
    forward = np.concatenate([real, imag], axis=0)
    weight = np.full((SPEC,), 2.0 / SPEC)
    weight[0] = weight[BLOCK] = 1.0 / SPEC
    inverse = (forward * weight[:, None]).T
    return (
        np.concatenate(split_in_two(forward), axis=1),
        np.concatenate(split_in_two(inverse), axis=0),
    )


def dot(left, right):
    return jnp.dot(left, right, preferred_element_type=F32)


def spectrum(forward, block):
    both = dot(forward, jnp.concatenate([block, block], axis=0))
    return both[:BLOCK], both[BLOCK:]


def inverse_of(inverse, real, imag):
    both = jnp.concatenate([real, imag], axis=0)
    high = both.astype(BF16)
    low = (both - high.astype(F32)).astype(BF16)
    terms = dot(inverse, high)
    return terms[:BLOCK] + terms[BLOCK:] + dot(inverse[:BLOCK], low)


def beside(first, second):
    def joined(a, b):
        return jnp.concatenate([a[:HALF] + b[:HALF], a[HALF:] - b[HALF:]], axis=0)

    return joined(first[0], second[0]), joined(first[1], second[1])


def first_row(shape):
    return lax.broadcasted_iota(jnp.int32, shape, 0) == 0


def product(left, right):
    return (left.astype(F32) * right.astype(F32)).astype(BF16)


def rows(block):
    return pl.ds(block * BLOCK, BLOCK)


def correlation_terms(grad, gated):
    real = grad[0] * gated[0]
    imag = grad[1] * gated[1]
    cross = grad[1] * gated[0] - grad[0] * gated[1]
    return real, imag, cross


def correlation(inverse, terms):
    real, imag, cross = terms
    top = first_row(real.shape)
    return inverse_of(
        inverse, real + jnp.where(top, 0.0, imag), jnp.where(top, imag, cross)
    )


def inner_kernel(gated_ref, mix_ref, fwd_ref, inv_ref, out_ref, edge_ref):
    fwd, inv = fwd_ref[...], inv_ref[...]
    blocks = gated_ref.shape[0] // BLOCK
    for part in range(gated_ref.shape[1] // WIDTH):
        chans = pl.ds(part * WIDTH, WIDTH)
        terms = None
        before = None
        for n in range(blocks):
            gated = spectrum(fwd, gated_ref[rows(n), chans])
            grad = spectrum(fwd, mix_ref[rows(n), chans])
            if n == 0:
                edge_ref[:BLOCK, chans], edge_ref[BLOCK:, chans] = grad
            window = gated if before is None else beside(gated, before)
            more = correlation_terms(grad, window)
            terms = more if terms is None else tuple(a + b for a, b in zip(terms, more))
            before = gated
        out_ref[:, chans] = correlation(inv, terms)


def outer_kernel(halo_ref, edge_ref, inner_ref, fwd_ref, inv_ref, out_ref):
    fwd, inv = fwd_ref[...], inv_ref[...]
    for part in range(halo_ref.shape[1] // WIDTH):
        chans = pl.ds(part * WIDTH, WIDTH)
        halo = spectrum(fwd, halo_ref[:, chans])
        window = [jnp.concatenate([a[:HALF], -a[HALF:]], axis=0) for a in halo]
        grad = edge_ref[:BLOCK, chans], edge_ref[BLOCK:, chans]
        total = inner_ref[:, chans] + correlation(inv, correlation_terms(grad, window))
        for piece in range(WIDTH // 128):
            out_ref[rows(part * (WIDTH // 128) + piece), :] = total[
                :, piece * 128 : (piece + 1) * 128
            ].astype(BF16)


def conv_kernel(
    gated_ref, mix_ref, key_ref, value_ref, grad_ref, before_ref, after_ref, taps_ref, fwd_ref, inv_ref,
    out_query_ref, out_key_ref, out_value_ref,
):
    fwd, inv = fwd_ref[...], inv_ref[...]
    blocks = gated_ref.shape[0] // BLOCK
    real, imag = spectrum(fwd, taps_ref[...])
    top = first_row(real.shape)
    cross = jnp.where(top, 0.0, imag)
    last = jnp.where(top, imag, real)

    def backward(n, grad, after):
        wr, wi = beside(grad, after)
        carried = inverse_of(inv, wr * real + wi * cross, wi * last - wr * cross)
        out_key_ref[0, rows(n), :] = (carried * value_ref[0, rows(n), :].astype(F32)).astype(BF16)
        out_value_ref[0, rows(n), :] = (carried * key_ref[0, rows(n), :].astype(F32)).astype(BF16)

    before = spectrum(fwd, before_ref[...])
    earlier = None
    for n in range(blocks):
        gated = spectrum(fwd, gated_ref[rows(n), :])
        grad = spectrum(fwd, mix_ref[rows(n), :])
        wr, wi = beside(gated, before)
        mixed = inverse_of(inv, wr * real - wi * cross, wr * cross + wi * last)
        out_query_ref[0, rows(n), :] = (grad_ref[0, rows(n), :].astype(F32) * mixed).astype(BF16)
        if earlier is not None:
            backward(n - 1, earlier, grad)
        before, earlier = gated, grad
    backward(blocks - 1, earlier, spectrum(fwd, after_ref[...]))


def params():
    return pltpu.CompilerParams(vmem_limit_bytes=VMEM_LIMIT)


def cost(flops, moved):
    return pl.CostEstimate(flops=flops, bytes_accessed=moved, transcendentals=0)


def shards(query_act, key_act, value_act, filter_taps, grad_out, count_all=1):
    _, row_count, chan_count = query_act.shape
    blocks = row_count // BLOCK
    fwd_np, inv_np = transform_matrices()
    fwd, inv = jnp.asarray(fwd_np), jnp.asarray(inv_np)

    whole = pl.BlockSpec((1, row_count, chan_count), lambda i: (0, 0, 0))
    stack = pl.BlockSpec((row_count, chan_count), lambda i: (0, 0))
    slab = pl.BlockSpec((BLOCK, chan_count), lambda i: (0, 0))
    fwd_spec = pl.BlockSpec(fwd.shape, lambda i: (0, 0))
    inv_spec = pl.BlockSpec(inv.shape, lambda i: (0, 0))

    gated = product(key_act[0], value_act[0])
    mix = product(query_act[0], grad_out[0])

    ctx = ("z", "xh", "c")
    ring = 1
    for name in ctx:
        ring *= lax.axis_size(name)
    gated_edge, mix_edge = gated[row_count - BLOCK :], mix[:BLOCK]
    first_core = lax.axis_index("c") == 0
    inside = [(i, i + 1) for i in range(0, ring - 1, 2)]
    outside = [(i, i + 1) for i in range(1, ring - 1, 2)]
    both_ways = [pairs + [(j, i) for i, j in pairs] for pairs in (inside, outside)]
    from_inside = lax.ppermute(jnp.where(first_core, gated_edge, mix_edge), ctx, both_ways[0])
    to_outside = jnp.where(
        first_core,
        product(query_act[0, :BLOCK], grad_out[0, :BLOCK]),
        product(key_act[0, row_count - BLOCK :], value_act[0, row_count - BLOCK :]),
    )
    from_outside = lax.ppermute(to_outside, ctx, both_ways[1])
    before = jnp.where(first_core, from_outside, from_inside)
    after = jnp.where(first_core, from_inside, from_outside)

    close = pl.BlockSpec(memory_space=pltpu.VMEM)
    inner, edge_spectrum = pl.pallas_call(
        inner_kernel,
        in_specs=[close] * 4,
        out_specs=[close] * 2,
        out_shape=[
            jax.ShapeDtypeStruct((BLOCK, chan_count), F32),
            jax.ShapeDtypeStruct((SPEC, chan_count), F32),
        ],
        compiler_params=params(),
        cost_estimate=cost(800_000_000, 2_500_000),
        name="inner_pairs",
    )(gated, mix, fwd, inv)

    partial = pl.pallas_call(
        outer_kernel,
        in_specs=[close] * 5,
        out_specs=close,
        out_shape=jax.ShapeDtypeStruct((BLOCK * chan_count // 128, 128), BF16),
        compiler_params=params(),
        cost_estimate=cost(200_000_000, 800_000),
        name="outer_pairs",
    )(before, edge_spectrum, inner, fwd, inv)

    near = ("c", "xh", "xl", "y")
    near_count = 1
    for name in near:
        near_count *= lax.axis_size(name)
    far = "z"
    far_count = lax.axis_size(far)
    chunks = partial.reshape(near_count, -1, 128)
    mine = lax.all_to_all(chunks, near, 0, 0, tiled=True).astype(F32).sum(axis=0)
    mine, before, after = lax.optimization_barrier((mine, before, after))
    out_shape = jax.ShapeDtypeStruct(query_act.shape, BF16)
    grad_query, grad_key, grad_value = pl.pallas_call(
        conv_kernel,
        grid=(1,),
        in_specs=[stack, stack, whole, whole, whole, slab, slab, slab, fwd_spec, inv_spec],
        out_specs=[whole, whole, whole],
        out_shape=[out_shape, out_shape, out_shape],
        compiler_params=params(),
        cost_estimate=cost(2_000_000_000, 4_000_000),
        name="convolutions",
    )(gated, mix, key_act, value_act, grad_out, before, after, filter_taps, fwd, inv)
    planes = jnp.broadcast_to(mine.astype(BF16)[None], (far_count,) + mine.shape)
    mine = lax.all_to_all(planes, far, 0, 0, tiled=True).astype(F32).sum(axis=0) / math.sqrt(count_all)
    mine, grad_query, grad_key, grad_value = lax.optimization_barrier(
        (mine, grad_query, grad_key, grad_value)
    )
    copies = jnp.broadcast_to(mine.astype(BF16)[None], (near_count,) + mine.shape)
    total = lax.all_to_all(copies, near, 0, 0, tiled=True)
    total = total.reshape(chan_count // 128, BLOCK, 128).astype(F32)
    grad_filter = jnp.concatenate([total[i] for i in range(chan_count // 128)], axis=1)

    return grad_query, grad_key, grad_value, grad_filter


def solution(mesh):
    fine = Mesh(mesh.devices.reshape(8, 2, 2, 4, 2), ("z", "xh", "c", "y", "xl"))
    spec = P(("y", "xl"), ("z", "xh", "c"), None)

    def whole(query_act, key_act, value_act, filter_taps, grad_out):
        count_all = query_act.shape[0] * query_act.shape[1]
        return jax.shard_map(
            functools.partial(shards, count_all=count_all),
            mesh=fine,
            in_specs=(spec, spec, spec, P(), spec),
            out_specs=(spec, spec, spec, P()),
            check_vma=False,
        )(query_act, key_act, value_act, filter_taps, grad_out)

    return whole
```
